32 devices in a mesh: parts: 2 (over x), inner: 16 (over z, y, core).
Axes of the slice: x: 2, y: 2, z: 4, core: 2. Of those that a mesh axis runs over, the one named last changes fastest.
Arguments:
- query_in: bfloat16 [4096, 2048], P(('parts', 'inner')), parts along dimension 0, may hold values from -6 to 6
- key_in: bfloat16 [4096, 2048], P(('parts', 'inner')), parts along dimension 0, may hold values from -6 to 6
- value_in: bfloat16 [4096, 2048], P(('parts', 'inner')), parts along dimension 0, may hold values from -6 to 6
- grad_out: bfloat16 [4096, 2048], P(('parts', 'inner')), parts along dimension 0, may hold values from -6 to 6
- filter_raw: float32 [2048, 2048], P('inner'), may hold values from -6 to 6
- decay_rate: float32 [2048], replicated, may hold values from 0.5 to 3
- short_weight: float32 [3, 2048], replicated, may hold values from -3.5 to 3.5
Outputs:
- grad_query: bfloat16 [4096, 2048], P(('parts', 'inner')), parts along dimension 0
- grad_key: bfloat16 [4096, 2048], P(('parts', 'inner')), parts along dimension 0
- grad_value: bfloat16 [4096, 2048], P(('parts', 'inner')), parts along dimension 0
- grad_filter: float32 [4096, 2048], P(('parts', 'inner')), parts along dimension 0
- grad_short: float32 [6, 2048], P('parts'), parts along dimension 0
The draws below stay inside these ranges and needn't reach their ends.
There are 2 independent parts, one for each index of `parts`. The reference program is written for one: setup_inputs(seed, part) draws one part's arguments, and reference() takes and returns one part's arrays. A program takes and returns all parts, laid end to end along the dimension named above; an argument that names none is the same for every part. Nothing has to cross between parts.
All inputs are finite; a program needn't handle non-finite values.
Results may differ from the reference program's by a relative error of at most 0.0085.
Values may be sent and summed in bfloat16 or wider, within the bound.
A program may use at most 128 MiB of HBM per device.

```python
import math
import jax
import jax.numpy as jnp
from jax import lax

C = 2048
TOKENS = 2048


def draw_filter_raw(key, part):
    key = jax.random.fold_in(key, 11)
    lag_line = jnp.arange(TOKENS, dtype=jnp.float32) / TOKENS
    levels = (0.3 * jnp.exp(jnp.log(5.0) * lag_line))[:, None]
    values_drawn = jnp.clip(jax.random.normal(key, (TOKENS, C), jnp.float32), -4.0, 4.0)
    return values_drawn * levels


def block_scale(rng, dims, cuts, least, high):
    def one(dim, shards_of):
        heights = jax.random.uniform(jax.random.fold_in(jax.random.fold_in(rng, 6), dim), (shards_of,), jnp.float32, least / len(cuts), high / len(cuts))
        return jnp.repeat(jnp.exp(heights), dims[dim] // shards_of).reshape((-1,) + (1,) * (len(dims) - dim - 1))

    level = one(*cuts[0])
    for cut in cuts[1:]:
        level = level * one(*cut)
    return level


def noise(rng, dims, spread, limit, cuts=(), kind=jnp.bfloat16):
    loudness = block_scale(rng, dims, cuts, -0.22, 0.18) if cuts else 1.0
    values = jax.random.normal(rng, dims, jnp.float32) * spread * loudness
    return jnp.minimum(jnp.maximum(values, -limit), limit).astype(kind)


def setup_inputs(seed: int = 0, part: int = 0) -> dict:
    streams_of = jax.random.split(jax.random.key(seed), 8)
    part_splits = jax.random.split(jax.random.fold_in(streams_of[7], part), 8)
    query_in = noise(part_splits[0], (TOKENS, C), 1.0, 6.0, ((0, 16),))
    key_in = noise(part_splits[1], (TOKENS, C), 1.0, 6.0, ((0, 16),))
    value_in = noise(part_splits[2], (TOKENS, C), 1.0, 6.0, ((0, 16),))
    grad_out = noise(part_splits[3], (TOKENS, C), 1.0, 6.0, ((0, 16),))
    filter_raw = draw_filter_raw(jax.random.fold_in(streams_of[7], 71), part)
    decay_rate = jnp.clip(jnp.exp(jax.random.uniform(streams_of[5], (C,), jnp.float32, math.log(0.5), math.log(3.0))), 0.5, 3.0)
    short_weight = noise(streams_of[6], (3, C), 3 ** -0.5, 3.5, (), jnp.float32)
    return {"query_in": query_in, "key_in": key_in, "value_in": value_in, "grad_out": grad_out, "filter_raw": filter_raw, "decay_rate": decay_rate, "short_weight": short_weight}


def reference(query_in, key_in, value_in, grad_out, filter_raw, decay_rate, short_weight):
    scale_factor = 1.0 / math.sqrt(TOKENS)
    value_now = value_in.astype(jnp.float32)
    zero_row = jnp.zeros((1, C), jnp.float32)
    value_one = jnp.concatenate([zero_row, value_now[:-1]], axis=0)
    value_two = jnp.concatenate([zero_row, zero_row, value_now[:-2]], axis=0)
    shaped_f = short_weight[0] * value_now + short_weight[1] * value_one + short_weight[2] * value_two
    shaped = shaped_f.astype(jnp.bfloat16)
    mixed = (key_in.astype(jnp.float32) * shaped.astype(jnp.float32)).astype(jnp.bfloat16)
    gated = (query_in.astype(jnp.float32) * grad_out.astype(jnp.float32)).astype(jnp.bfloat16)
    position = jnp.arange(TOKENS, dtype=jnp.float32)
    envelope = jnp.exp(-decay_rate[None, :] * position[:, None] / TOKENS) * scale_factor
    lagged = filter_raw * envelope

    def to_blocks(array):
        return array.reshape(TOKENS, C // 128, 128).transpose(1, 0, 2)

    def from_blocks(array):
        return array.transpose(1, 0, 2).reshape(TOKENS, C)

    def spectral(items):
        mixed_block, gated_block, filter_block = items
        fft_length = 2 * TOKENS
        spec_mixed = jnp.fft.rfft(mixed_block, n=fft_length, axis=0)
        spec_gated = jnp.fft.rfft(gated_block, n=fft_length, axis=0)
        spec_filter = jnp.fft.rfft(filter_block, n=fft_length, axis=0)
        conv_block = jnp.fft.irfft(spec_filter * spec_mixed, n=fft_length, axis=0)[:TOKENS]
        grad_block = jnp.fft.irfft(jnp.conj(spec_filter) * spec_gated, n=fft_length, axis=0)[:TOKENS]
        lag_block = jnp.fft.irfft(spec_gated * jnp.conj(spec_mixed), n=fft_length, axis=0)[:TOKENS]
        return (conv_block, grad_block, lag_block)
    conv_blocks, grad_blocks, lag_blocks = lax.map(spectral, (to_blocks(mixed.astype(jnp.float32)), to_blocks(gated.astype(jnp.float32)), to_blocks(lagged)))
    conv = from_blocks(conv_blocks).astype(jnp.bfloat16)
    grad_mixed = from_blocks(grad_blocks).astype(jnp.bfloat16)
    grad_lag = from_blocks(lag_blocks)
    grad_query = (grad_out.astype(jnp.float32) * conv.astype(jnp.float32)).astype(jnp.bfloat16)
    grad_key = (grad_mixed.astype(jnp.float32) * shaped.astype(jnp.float32)).astype(jnp.bfloat16)
    grad_shaped = (grad_mixed.astype(jnp.float32) * key_in.astype(jnp.float32)).astype(jnp.bfloat16)
    grad_now = grad_shaped.astype(jnp.float32)
    grad_one = jnp.concatenate([grad_now[1:], zero_row], axis=0)
    grad_two = jnp.concatenate([grad_now[2:], zero_row, zero_row], axis=0)
    grad_value = (short_weight[0] * grad_now + short_weight[1] * grad_one + short_weight[2] * grad_two).astype(jnp.bfloat16)
    grad_short = jnp.stack([lax.optimization_barrier(jnp.sum(grad_now * value_now, axis=0)), lax.optimization_barrier(jnp.sum(grad_now * value_one, axis=0)), lax.optimization_barrier(jnp.sum(grad_now * value_two, axis=0))]) * scale_factor
    grad_filter = grad_lag * envelope
    return (grad_query, grad_key, grad_value, grad_filter, grad_short)
```

```python
import functools
import math

import jax
import jax.numpy as jnp
import ml_dtypes
import numpy as np
from jax import lax
from jax.experimental import pallas as pl
from jax.experimental.pallas import tpu as pltpu
from jax.sharding import PartitionSpec as P

HIGHEST = lax.Precision.HIGHEST
MESH = pl.DeviceIdType.MESH
F32 = jnp.float32
BF16 = jnp.bfloat16
THETA = 0.25
LANES = 128
CHUNK = 16


def inner_tables(group, rows):
    length = group * rows
    coarse = np.arange(group)[:, None, None]
    fine = np.arange(rows)[None, :, None]
    token = np.arange(rows)[None, None, :]
    angle = 2.0 * np.pi * token * (coarse + THETA + group * fine) / length
    cos, sin = np.cos(angle), np.sin(angle)
    forward = np.concatenate(
        [np.concatenate([cos, sin], axis=2), np.concatenate([-sin, cos], axis=2)], axis=1
    )
    backward = np.swapaxes(forward, 1, 2) / length
    return forward.astype(ml_dtypes.bfloat16), backward.astype(ml_dtypes.bfloat16)


def turn(value, angle):
    re, im = value
    cos, sin = math.cos(angle), math.sin(angle)
    if abs(sin) < 1e-12:
        return (re, im) if cos > 0 else (-re, -im)
    if abs(cos) < 1e-12:
        return (-im, re) if sin > 0 else (im, -re)
    if abs(abs(cos) - abs(sin)) < 1e-12:
        cs, sn = math.copysign(1, cos), math.copysign(1, sin)
        size = abs(cos)
        real = (re if cs > 0 else -re) - (im if sn > 0 else -im)
        imag = (im if cs > 0 else -im) + (re if sn > 0 else -re)
        return (real * size, imag * size)
    return (re * cos - im * sin, im * cos + re * sin)


def small_transform(values, sign):
    count = len(values)
    if count == 1:
        return values
    even = small_transform(values[0::2], sign)
    odd = small_transform(values[1::2], sign)
    half = count // 2
    low, high = [], []
    for k in range(half):
        a = even[k]
        b = turn(odd[k], sign * 2.0 * math.pi * k / count)
        low.append((a[0] + b[0], a[1] + b[1]))
        high.append((a[0] - b[0], a[1] - b[1]))
    return low + high


def outer_forward(group, source, target, row0, columns):
    rows = source.shape[1]

    def chunk(i, carry):
        at = pl.ds(pl.multiple_of(i * CHUNK, CHUNK), CHUNK)
        values = []
        for a in range(group):
            x = source[a, at, :].astype(F32)
            angle = -2.0 * math.pi * a * THETA / group
            values.append((x * math.cos(angle), x * math.sin(angle)))
        for k, (re, im) in enumerate(small_transform(values, -1.0)):
            target[k, at, columns] = re.astype(BF16)
            later = pl.ds(pl.multiple_of(rows + i * CHUNK, CHUNK), CHUNK)
            target[k, later, columns] = im.astype(BF16)
        return carry

    lax.fori_loop(0, rows // CHUNK, chunk, 0)


def outer_backward(group, source, columns, target):
    rows = target.shape[1]

    def chunk(i, carry):
        at = pl.ds(pl.multiple_of(i * CHUNK, CHUNK), CHUNK)
        later = pl.ds(pl.multiple_of(rows + i * CHUNK, CHUNK), CHUNK)
        values = [(source[k, at, columns], source[k, later, columns]) for k in range(group)]
        for a, (re, im) in enumerate(small_transform(values, 1.0)):
            angle = 2.0 * math.pi * a * THETA / group
            target[a, at, :] = (re * math.cos(angle) - im * math.sin(angle)).astype(BF16)
        return carry

    lax.fori_loop(0, rows // CHUNK, chunk, 0)


def kernel(
    group,
    query, key, value, grad, filt, decay, taps, table_f_hbm, table_b_hbm,
    out_query, out_key, out_value, out_filter, out_short,
    table_f, table_b, stage, recv, shaped, lines, spectra, waves,
    back, home, shaped_grad, rim_value, rim_grad, tap_part, tap_recv, tap_sum, tap_all,
    table_sem, send_sem, recv_sem, back_send, back_recv,
    rim_send, rim_recv, tap_send, tap_rsem, sum_send, sum_recv,
):
    rows = query.shape[0]
    length = rows * group
    scale = 1.0 / math.sqrt(length)
    me = lax.axis_index("inner")
    right, left = lax.rem(me + 1, group), lax.rem(me + group - 1, group)

    load_f = pltpu.make_async_copy(table_f_hbm, table_f, table_sem.at[0])
    load_b = pltpu.make_async_copy(table_b_hbm, table_b, table_sem.at[1])
    load_f.start()
    load_b.start()

    barrier = pltpu.get_barrier_semaphore()

    def greet(s, carry):
        pl.semaphore_signal(
            barrier, inc=1, device_id={"inner": lax.rem(me + s, group)}, device_id_type=MESH
        )
        return carry

    lax.fori_loop(1, group, greet, 0)

    def cols(p):
        return pl.ds(pl.multiple_of(p * LANES, LANES), LANES)

    def remote(src, dst, send, receive, device):
        return pltpu.make_async_remote_copy(
            src_ref=src, dst_ref=dst, send_sem=send, recv_sem=receive,
            device_id={"inner": device}, device_id_type=MESH,
        )

    def forward_copy(kind, s):
        peer = lax.rem(me + s, group)
        return remote(
            stage.at[kind, peer], recv.at[kind, me],
            send_sem.at[kind, s], recv_sem.at[kind, s], peer,
        )

    def back_copy(kind, s):
        peer = lax.rem(me + s, group)
        return remote(
            back.at[kind, peer], home.at[kind, me],
            back_send.at[kind, s], back_recv.at[kind, s], peer,
        )

    def envelope(p):
        line = lax.broadcasted_iota(jnp.int32, (rows, LANES), 0) + me * rows
        return jnp.exp(-decay[:, cols(p)] * line.astype(F32) / length) * scale

    def make_gated(p):
        return (query[:, cols(p)].astype(F32) * grad[:, cols(p)].astype(F32)).astype(BF16)

    def extended(p):
        rim = rim_value[:, cols(p)].astype(F32)
        rim = jnp.where(me == 0, jnp.zeros_like(rim), rim)
        ext = jnp.concatenate([rim, value[:, cols(p)].astype(F32)], axis=0)
        return ext[CHUNK:], ext[CHUNK - 1 : CHUNK - 1 + rows], ext[CHUNK - 2 : CHUNK - 2 + rows]

    def make_mixed(p):
        now, one, two = extended(p)
        weight = taps[:, cols(p)]
        low = (weight[0:1] * now + weight[1:2] * one + weight[2:3] * two).astype(BF16)
        shaped[p] = low
        return (key[:, cols(p)].astype(F32) * low.astype(F32)).astype(BF16)

    def make_lagged(p):
        return (filt[:, cols(p)] * envelope(p)).astype(BF16)

    def fill_own(kind, make):
        recv[kind, me] = make(me)

    def send_all(kind, make):
        def step(s, carry):
            peer = lax.rem(me + s, group)
            stage[kind, peer] = make(peer)
            forward_copy(kind, s).start()
            return carry

        lax.fori_loop(1, group, step, 0)

    fill_own(0, make_gated)
    fill_own(2, make_lagged)
    pl.semaphore_wait(barrier, group - 1)

    rim_copy = remote(
        value.at[pl.ds(rows - CHUNK, CHUNK), :], rim_value, rim_send.at[0], rim_recv.at[0], right
    )
    rim_copy.start()
    send_all(0, make_gated)
    rim_copy.wait_recv()
    send_all(1, make_mixed)
    fill_own(1, make_mixed)
    send_all(2, make_lagged)

    def await_all(copy, kind):
        def step(s, carry):
            copy(kind, s).wait_recv()
            return carry

        lax.fori_loop(1, group, step, 0)

    low, high = pl.ds(0, LANES), pl.ds(LANES, LANES)
    await_all(forward_copy, 0)
    outer_forward(group, recv.at[0], lines, 0, low)
    await_all(forward_copy, 1)
    outer_forward(group, recv.at[1], lines, 0, high)
    load_f.wait()
    load_b.wait()

    def lag_step(k, carry):
        both = jnp.dot(table_f[k], lines[k], preferred_element_type=F32)
        spectra[k] = both
        g_re, g_im = both[:rows, :LANES], both[rows:, :LANES]
        m_re, m_im = both[:rows, LANES:], both[rows:, LANES:]
        product = jnp.concatenate(
            [g_re * m_re + g_im * m_im, g_im * m_re - g_re * m_im], axis=0
        ).astype(BF16)
        waves[k, :, low] = jnp.dot(table_b[k], product, preferred_element_type=F32)
        return carry

    lax.fori_loop(0, group, lag_step, 0)
    outer_backward(group, waves, low, back.at[2])

    def return_all(kind):
        def step(s, carry):
            back_copy(kind, s).start()
            return carry

        lax.fori_loop(1, group, step, 0)

    return_all(2)

    await_all(forward_copy, 2)
    outer_forward(group, recv.at[2], lines, 0, low)

    def conv_step(k, carry):
        own = jnp.dot(table_f[k], lines[k, :, low], preferred_element_type=F32)
        l_re, l_im = own[:rows], own[rows:]
        both = spectra[k]
        g_re, g_im = both[:rows, :LANES], both[rows:, :LANES]
        m_re, m_im = both[:rows, LANES:], both[rows:, LANES:]
        grad_part = jnp.concatenate(
            [l_re * g_re + l_im * g_im, l_re * g_im - l_im * g_re], axis=0
        ).astype(BF16)
        conv_part = jnp.concatenate(
            [l_re * m_re - l_im * m_im, l_re * m_im + l_im * m_re], axis=0
        ).astype(BF16)
        product = jnp.concatenate([grad_part, conv_part], axis=1)
        waves[k] = jnp.dot(table_b[k], product, preferred_element_type=F32)
        return carry

    lax.fori_loop(0, group, conv_step, 0)
    outer_backward(group, waves, low, back.at[0])
    return_all(0)
    outer_backward(group, waves, high, back.at[1])
    return_all(1)

    def keep_own(kind):
        home[kind, me] = back[kind, me]

    keep_own(2)
    keep_own(0)
    keep_own(1)

    await_all(back_copy, 2)

    def filter_step(p, carry):
        out_filter[:, cols(p)] = home[2, p].astype(F32) * envelope(p)
        return carry

    lax.fori_loop(0, group, filter_step, 0)

    await_all(back_copy, 0)

    def grad_step(p, carry):
        mixed_grad = home[0, p].astype(F32)
        out_key[:, cols(p)] = (mixed_grad * shaped[p].astype(F32)).astype(BF16)
        low_grad = (mixed_grad * key[:, cols(p)].astype(F32)).astype(BF16)
        shaped_grad[p] = low_grad
        line = low_grad.astype(F32)
        now, one, two = extended(p)
        sums = [jnp.sum(line * x, axis=0, keepdims=True) for x in (now, one, two)]
        tap_part[p] = jnp.concatenate(sums + [jnp.zeros((5, LANES), F32)], axis=0)
        return carry

    lax.fori_loop(0, group, grad_step, 0)
    rim_back = remote(
        shaped_grad.at[:, pl.ds(0, CHUNK), :], rim_grad, rim_send.at[1], rim_recv.at[1], left
    )
    rim_back.start()

    def tap_copy(s):
        peer = lax.rem(me + s, group)
        return remote(tap_part.at[peer], tap_recv.at[me], tap_send.at[s], tap_rsem.at[s], peer)

    def sum_copy(s):
        peer = lax.rem(me + s, group)
        return remote(tap_sum, tap_all.at[me], sum_send.at[s], sum_recv.at[s], peer)

    def loop(body):
        def step(s, carry):
            body(s)
            return carry

        lax.fori_loop(1, group, step, 0)

    loop(lambda s: tap_copy(s).start())
    tap_recv[me] = tap_part[me]
    rim_back.wait_recv()

    def value_step(p, carry):
        rim = rim_grad[p].astype(F32)
        rim = jnp.where(me == group - 1, jnp.zeros_like(rim), rim)
        ext = jnp.concatenate([shaped_grad[p].astype(F32), rim], axis=0)
        weight = taps[:, cols(p)]
        total = weight[0:1] * ext[:rows] + weight[1:2] * ext[1 : rows + 1]
        out_value[:, cols(p)] = (total + weight[2:3] * ext[2 : rows + 2]).astype(BF16)
        return carry

    lax.fori_loop(0, group, value_step, 0)
    loop(lambda s: tap_copy(s).wait_recv())
    tap_sum[...] = jnp.sum(tap_recv[...], axis=0) * scale
    loop(lambda s: sum_copy(s).start())
    tap_all[me] = tap_sum[...]

    await_all(back_copy, 1)

    def query_step(p, carry):
        conv = home[1, p].astype(F32)
        out_query[:, cols(p)] = (grad[:, cols(p)].astype(F32) * conv).astype(BF16)
        return carry

    lax.fori_loop(0, group, query_step, 0)
    loop(lambda s: sum_copy(s).wait_recv())
    for p in range(group):
        out_short[:, p * LANES : (p + 1) * LANES] = tap_all[p][0:3]

    def drain(s):
        for kind in range(3):
            forward_copy(kind, s).wait_send()
            back_copy(kind, s).wait_send()
        tap_copy(s).wait_send()
        sum_copy(s).wait_send()

    loop(drain)
    rim_copy.wait_send()
    rim_back.wait_send()


def fused(group, query_in, key_in, value_in, grad_out, filter_raw, decay_rate, short_weight):
    rows, channels = query_in.shape
    table_f, table_b = inner_tables(group, rows)
    vmem = pl.BlockSpec(memory_space=pltpu.VMEM)
    blocks = (group, rows, LANES)
    dma = pltpu.SemaphoreType.DMA
    return pl.pallas_call(
        functools.partial(kernel, group),
        out_shape=(
            jax.ShapeDtypeStruct((rows, channels), BF16),
            jax.ShapeDtypeStruct((rows, channels), BF16),
            jax.ShapeDtypeStruct((rows, channels), BF16),
            jax.ShapeDtypeStruct((rows, channels), F32),
            jax.ShapeDtypeStruct((3, channels), F32),
        ),
        in_specs=[vmem] * 7 + [pl.BlockSpec(memory_space=pl.ANY)] * 2,
        out_specs=(vmem,) * 5,
        scratch_shapes=[
            pltpu.VMEM(table_f.shape, BF16),
            pltpu.VMEM(table_b.shape, BF16),
            pltpu.VMEM((3,) + blocks, BF16),
            pltpu.VMEM((3,) + blocks, BF16),
            pltpu.VMEM(blocks, BF16),
            pltpu.VMEM((group, 2 * rows, 2 * LANES), BF16),
            pltpu.VMEM((group, 2 * rows, 2 * LANES), F32),
            pltpu.VMEM((group, 2 * rows, 2 * LANES), F32),
            pltpu.VMEM((3,) + blocks, BF16),
            pltpu.VMEM((3,) + blocks, BF16),
            pltpu.VMEM(blocks, BF16),
            pltpu.VMEM((CHUNK, channels), BF16),
            pltpu.VMEM((group, CHUNK, LANES), BF16),
            pltpu.VMEM((group, 8, LANES), F32),
            pltpu.VMEM((group, 8, LANES), F32),
            pltpu.VMEM((8, LANES), F32),
            pltpu.VMEM((group, 8, LANES), F32),
            dma((2,)),
            dma((3, group)),
            dma((3, group)),
            dma((3, group)),
            dma((3, group)),
            dma((2,)),
            dma((2,)),
            dma((group,)),
            dma((group,)),
            dma((group,)),
            dma((group,)),
        ],
        compiler_params=pltpu.CompilerParams(
            collective_id=0, has_side_effects=True, vmem_limit_bytes=56 * 2**20
        ),
    )(
        query_in, key_in, value_in, grad_out, filter_raw,
        decay_rate.reshape(1, channels), short_weight,
        jnp.asarray(table_f), jnp.asarray(table_b),
    )


def shifted(block, axis, distance):
    devices = range(lax.axis_size(axis))
    route = [(i - distance, i) for i in devices if i - distance in devices]
    return lax.ppermute(block, axis, route)


def dft_tables(length):
    index_line = jnp.arange(length, dtype=jnp.int32)
    phase_int = index_line[:, None] * index_line[None, :] % length
    angles = phase_int.astype(jnp.float32) * (-2.0 * math.pi / length)
    return (jnp.cos(angles), jnp.sin(angles))


def twist_tables(outer_size, inner_size, length):
    outer_line = jnp.arange(outer_size, dtype=jnp.int32)
    inner_line = jnp.arange(inner_size, dtype=jnp.int32)
    phase_int = outer_line[:, None] * inner_line[None, :] % length
    angles = phase_int.astype(jnp.float32) * (-2.0 * math.pi / length)
    return (jnp.cos(angles), jnp.sin(angles))


def right_multiply(values, table):
    return jnp.einsum("ckn,nm->ckm", values, table, precision=HIGHEST)


def forward_transform(signal, tables):
    cos_outer, sin_outer, cos_inner, sin_inner, twist_cos, twist_sin = tables
    channels = signal.shape[0]
    half_rows = cos_outer.shape[0] // 2
    blocks = signal.reshape(channels, half_rows, cos_inner.shape[0])
    first_re = jnp.einsum("kn,cna->cka", cos_outer[:, :half_rows], blocks, precision=HIGHEST)
    first_im = jnp.einsum("kn,cna->cka", sin_outer[:, :half_rows], blocks, precision=HIGHEST)
    turned_re = first_re * twist_cos - first_im * twist_sin
    turned_im = first_re * twist_sin + first_im * twist_cos
    spec_re = right_multiply(turned_re, cos_inner) - right_multiply(turned_im, sin_inner)
    spec_im = right_multiply(turned_re, sin_inner) + right_multiply(turned_im, cos_inner)
    return (spec_re, spec_im)


def inverse_transform(spec_re, spec_im, tables):
    cos_outer, sin_outer, cos_inner, sin_inner, twist_cos, twist_sin = tables
    channels = spec_re.shape[0]
    half_rows = cos_outer.shape[0] // 2
    back_re = right_multiply(spec_re, cos_inner) + right_multiply(spec_im, sin_inner)
    back_im = right_multiply(spec_im, cos_inner) - right_multiply(spec_re, sin_inner)
    turned_re = back_re * twist_cos + back_im * twist_sin
    turned_im = back_im * twist_cos - back_re * twist_sin
    signal = jnp.einsum("nk,cka->cna", cos_outer[:half_rows], turned_re, precision=HIGHEST)
    signal = signal + jnp.einsum("nk,cka->cna", sin_outer[:half_rows], turned_im, precision=HIGHEST)
    scaled = signal * (1.0 / (cos_outer.shape[0] * cos_inner.shape[0]))
    return scaled.reshape(channels, -1)


def per_device(query_in, key_in, value_in, grad_out, filter_raw, decay_rate, short_weight):
    local_rows = query_in.shape[0]
    group_size = lax.axis_size("inner")
    seq_length = local_rows * group_size
    scale_factor = 1.0 / math.sqrt(seq_length)
    first_row = lax.axis_index("inner") * local_rows
    position = (first_row + jnp.arange(local_rows, dtype=jnp.int32)).astype(jnp.float32)
    envelope = jnp.exp(-decay_rate[None, :] * position[:, None] / seq_length) * scale_factor
    rim_rows = shifted(value_in[local_rows - 2 :], "inner", 1)
    extended = jnp.concatenate([rim_rows, value_in], axis=0).astype(jnp.float32)
    value_now = extended[2:]
    value_one = extended[1:-1]
    value_two = extended[:-2]
    shaped = (
        short_weight[0] * value_now + short_weight[1] * value_one + short_weight[2] * value_two
    ).astype(jnp.bfloat16)
    mixed = (key_in.astype(jnp.float32) * shaped.astype(jnp.float32)).astype(jnp.bfloat16)
    gated = (query_in.astype(jnp.float32) * grad_out.astype(jnp.float32)).astype(jnp.bfloat16)
    lagged = filter_raw * envelope
    mixed_half, gated_half = (
        lax.all_to_all(mixed.T, "inner", split_axis=0, concat_axis=1, tiled=True),
        lax.all_to_all(gated.T, "inner", split_axis=0, concat_axis=1, tiled=True),
    )
    filter_cols = lax.all_to_all(lagged.T, "inner", split_axis=0, concat_axis=1, tiled=True)
    mixed_cols = mixed_half.astype(jnp.float32)
    gated_cols = gated_half.astype(jnp.float32)
    fft_length = 2 * seq_length
    exponent = fft_length.bit_length() - 1
    inner_size = 2 ** (exponent // 2)
    outer_size = fft_length // inner_size
    cos_outer, sin_outer = dft_tables(outer_size)
    cos_inner, sin_inner = dft_tables(inner_size)
    twist_cos, twist_sin = twist_tables(outer_size, inner_size, fft_length)
    tables = (cos_outer, sin_outer, cos_inner, sin_inner, twist_cos, twist_sin)
    mix_re, mix_im = forward_transform(mixed_cols, tables)
    gate_re, gate_im = forward_transform(gated_cols, tables)
    filt_re, filt_im = forward_transform(filter_cols, tables)
    conv_cols = inverse_transform(
        filt_re * mix_re - filt_im * mix_im, filt_re * mix_im + filt_im * mix_re, tables
    )
    grad_cols = inverse_transform(
        filt_re * gate_re + filt_im * gate_im, filt_re * gate_im - filt_im * gate_re, tables
    )
    lag_cols = inverse_transform(
        gate_re * mix_re + gate_im * mix_im, gate_im * mix_re - gate_re * mix_im, tables
    )
    conv_low = conv_cols.astype(jnp.bfloat16)
    grad_low = grad_cols.astype(jnp.bfloat16)
    conv_rows, grad_rows = (
        lax.all_to_all(conv_low, "inner", split_axis=1, concat_axis=0, tiled=True),
        lax.all_to_all(grad_low, "inner", split_axis=1, concat_axis=0, tiled=True),
    )
    lag_rows = lax.all_to_all(lag_cols, "inner", split_axis=1, concat_axis=0, tiled=True)
    conv = conv_rows.T.astype(jnp.float32)
    grad_mixed = grad_rows.T.astype(jnp.float32)
    grad_lag = lag_rows.T
    grad_query = (grad_out.astype(jnp.float32) * conv).astype(jnp.bfloat16)
    grad_key = (grad_mixed * shaped.astype(jnp.float32)).astype(jnp.bfloat16)
    grad_shaped = (grad_mixed * key_in.astype(jnp.float32)).astype(jnp.bfloat16)
    next_rows = shifted(grad_shaped[:2], "inner", -1)
    grad_ext = jnp.concatenate([grad_shaped, next_rows], axis=0).astype(jnp.float32)
    grad_now = grad_ext[:local_rows]
    grad_one = grad_ext[1 : local_rows + 1]
    grad_two = grad_ext[2:]
    grad_value = (
        short_weight[0] * grad_now + short_weight[1] * grad_one + short_weight[2] * grad_two
    ).astype(jnp.bfloat16)
    partial_taps = jnp.stack(
        [
            jnp.sum(grad_now * value_now, axis=0),
            jnp.sum(grad_now * value_one, axis=0),
            jnp.sum(grad_now * value_two, axis=0),
        ]
    )
    grad_short = lax.psum(partial_taps, "inner") * scale_factor
    grad_filter = grad_lag * envelope
    return (grad_query, grad_key, grad_value, grad_filter, grad_short)


def dispatch(*arrays):
    rows, channels = arrays[0].shape
    group = lax.axis_size("inner")
    if rows == LANES and group == 16 and channels == group * LANES:
        return fused(group, *arrays)
    return per_device(*arrays)


def solution(mesh):
    in_specs = (
        P(("parts", "inner"), None),
        P(("parts", "inner"), None),
        P(("parts", "inner"), None),
        P(("parts", "inner"), None),
        P("inner", None),
        P(),
        P(),
    )
    out_specs = (
        P(("parts", "inner"), None),
        P(("parts", "inner"), None),
        P(("parts", "inner"), None),
        P(("parts", "inner"), None),
        P("parts", None),
    )
    return jax.shard_map(
        dispatch, mesh=mesh, in_specs=in_specs, out_specs=out_specs, check_vma=False
    )
```

```python
import functools
import math

import jax
import jax.numpy as jnp
import ml_dtypes
import numpy as np
from jax import lax
from jax.experimental import pallas as pl
from jax.experimental.pallas import tpu as pltpu
from jax.sharding import PartitionSpec as P

HIGHEST = lax.Precision.HIGHEST
MESH = pl.DeviceIdType.MESH
F32 = jnp.float32
BF16 = jnp.bfloat16
THETA = 0.25
LANES = 128
CHUNK = 16
CUT_ONE, CUT_TWO = 8, 13


def inner_tables(group, rows):
    length = group * rows
    coarse = np.arange(group)[:, None, None]
    fine = np.arange(rows)[None, :, None]
    token = np.arange(rows)[None, None, :]
    angle = 2.0 * np.pi * token * (coarse + THETA + group * fine) / length
    cos, sin = np.cos(angle), np.sin(angle)
    forward = np.concatenate(
        [np.concatenate([cos, sin], axis=2), np.concatenate([-sin, cos], axis=2)], axis=1
    )
    backward = np.swapaxes(forward, 1, 2) / length
    return forward.astype(ml_dtypes.bfloat16), backward.astype(ml_dtypes.bfloat16)


def turn(value, angle):
    re, im = value
    cos, sin = math.cos(angle), math.sin(angle)
    if abs(sin) < 1e-12:
        return (re, im) if cos > 0 else (-re, -im)
    if abs(cos) < 1e-12:
        return (-im, re) if sin > 0 else (im, -re)
    if abs(abs(cos) - abs(sin)) < 1e-12:
        cs, sn = math.copysign(1, cos), math.copysign(1, sin)
        size = abs(cos)
        real = (re if cs > 0 else -re) - (im if sn > 0 else -im)
        imag = (im if cs > 0 else -im) + (re if sn > 0 else -re)
        return (real * size, imag * size)
    return (re * cos - im * sin, im * cos + re * sin)


def small_transform(values, sign):
    count = len(values)
    if count == 1:
        return values
    even = small_transform(values[0::2], sign)
    odd = small_transform(values[1::2], sign)
    half = count // 2
    low, high = [], []
    for k in range(half):
        a = even[k]
        b = turn(odd[k], sign * 2.0 * math.pi * k / count)
        low.append((a[0] + b[0], a[1] + b[1]))
        high.append((a[0] - b[0], a[1] - b[1]))
    return low + high


def outer_forward(group, source, target, row0, columns):
    rows = source.shape[1]

    def chunk(i, carry):
        at = pl.ds(pl.multiple_of(i * CHUNK, CHUNK), CHUNK)
        values = []
        for a in range(group):
            x = source[a, at, :].astype(F32)
            angle = -2.0 * math.pi * a * THETA / group
            values.append((x * math.cos(angle), x * math.sin(angle)))
        for k, (re, im) in enumerate(small_transform(values, -1.0)):
            target[k, at, columns] = re.astype(BF16)
            later = pl.ds(pl.multiple_of(rows + i * CHUNK, CHUNK), CHUNK)
            target[k, later, columns] = im.astype(BF16)
        return carry

    lax.fori_loop(0, rows // CHUNK, chunk, 0)


def outer_backward(group, source, columns, target):
    rows = target.shape[1]

    def chunk(i, carry):
        at = pl.ds(pl.multiple_of(i * CHUNK, CHUNK), CHUNK)
        later = pl.ds(pl.multiple_of(rows + i * CHUNK, CHUNK), CHUNK)
        values = [(source[k, at, columns], source[k, later, columns]) for k in range(group)]
        for a, (re, im) in enumerate(small_transform(values, 1.0)):
            angle = 2.0 * math.pi * a * THETA / group
            target[a, at, :] = (re * math.cos(angle) - im * math.sin(angle)).astype(BF16)
        return carry

    lax.fori_loop(0, rows // CHUNK, chunk, 0)


def kernel(
    group,
    query, key, value, grad, filt, decay, taps, table_f_hbm, table_b_hbm,
    out_query, out_key, out_value, out_filter, out_short,
    table_f, table_b, stage, recv, shaped, lines, spectra, waves,
    back, home, shaped_grad, rim_value, rim_grad, tap_part, tap_recv, tap_sum, tap_all,
    table_sem, send_sem, recv_sem, back_send, back_recv,
    rim_send, rim_recv, tap_send, tap_rsem, sum_send, sum_recv, twin_send, twin_recv,
):
    rows = query.shape[0]
    length = rows * group
    scale = 1.0 / math.sqrt(length)
    me = lax.axis_index("inner")
    right, left = lax.rem(me + 1, group), lax.rem(me + group - 1, group)

    load_f = pltpu.make_async_copy(table_f_hbm, table_f, table_sem.at[0])
    load_b = pltpu.make_async_copy(table_b_hbm, table_b, table_sem.at[1])
    load_f.start()
    load_b.start()

    barrier = pltpu.get_barrier_semaphore()

    def greet(s, carry):
        pl.semaphore_signal(
            barrier, inc=1, device_id={"inner": lax.rem(me + s, group)}, device_id_type=MESH
        )
        return carry

    lax.fori_loop(1, group, greet, 0)
    part = lax.axis_index("parts")
    pl.semaphore_signal(barrier, inc=1, device_id={"parts": 1 - part}, device_id_type=MESH)

    def cols(p):
        return pl.ds(pl.multiple_of(p * LANES, LANES), LANES)

    def remote(src, dst, send, receive, device):
        return pltpu.make_async_remote_copy(
            src_ref=src, dst_ref=dst, send_sem=send, recv_sem=receive,
            device_id={"inner": device}, device_id_type=MESH,
        )

    def partner(s):
        distance = lax.rem(s, 2) * (group // 2) + s // 2
        peer = 0
        for bit in range(group.bit_length() - 1):
            place = 2**bit
            peer += place * lax.rem(me // place + distance // place, 2)
        return peer

    def ours(s):
        return lax.rem(s // 2, 2) == part

    def forward_copy(kind, s):
        peer = partner(s)
        return remote(
            stage.at[kind, peer], recv.at[kind, me],
            send_sem.at[kind, s], recv_sem.at[kind, s], peer,
        )

    def back_copy(kind, s):
        peer = partner(s)
        return remote(
            back.at[kind, peer], home.at[kind, me],
            back_send.at[kind, s], back_recv.at[kind, s], peer,
        )

    def envelope(p):
        line = lax.broadcasted_iota(jnp.int32, (rows, LANES), 0) + me * rows
        return jnp.exp(-decay[:, cols(p)] * line.astype(F32) / length) * scale

    def make_gated(p):
        return (query[:, cols(p)].astype(F32) * grad[:, cols(p)].astype(F32)).astype(BF16)

    def extended(p):
        rim = rim_value[:, cols(p)].astype(F32)
        rim = jnp.where(me == 0, jnp.zeros_like(rim), rim)
        ext = jnp.concatenate([rim, value[:, cols(p)].astype(F32)], axis=0)
        return ext[CHUNK:], ext[CHUNK - 1 : CHUNK - 1 + rows], ext[CHUNK - 2 : CHUNK - 2 + rows]

    def make_mixed(p):
        now, one, two = extended(p)
        weight = taps[:, cols(p)]
        low = (weight[0:1] * now + weight[1:2] * one + weight[2:3] * two).astype(BF16)
        shaped[p] = low
        return (key[:, cols(p)].astype(F32) * low.astype(F32)).astype(BF16)

    def make_lagged(p):
        return (filt[:, cols(p)] * envelope(p)).astype(BF16)

    def fill_own(kind, make):
        recv[kind, me] = make(me)

    def send_all(kind, make):
        def step(s, carry):
            peer = partner(s)
            stage[kind, peer] = make(peer)
            forward_copy(kind, s).start()
            return carry

        lax.fori_loop(1, group, step, 0)

    fill_own(0, make_gated)
    fill_own(2, make_lagged)
    pl.semaphore_wait(barrier, group)

    rim_copy = remote(
        value.at[pl.ds(rows - CHUNK, CHUNK), :], rim_value, rim_send.at[0], rim_recv.at[0], right
    )
    rim_copy.start()
    send_all(0, make_gated)
    rim_copy.wait_recv()
    send_all(1, make_mixed)
    fill_own(1, make_mixed)

    def send_filter(s, carry):
        @pl.when(ours(s))
        def _():
            peer = partner(s)
            stage[2, peer] = make_lagged(peer)
            forward_copy(2, s).start()

        return carry

    lax.fori_loop(1, group, send_filter, 0)

    def twin_copy(source):
        return pltpu.make_async_remote_copy(
            src_ref=recv.at[2, source], dst_ref=recv.at[2, source],
            send_sem=twin_send.at[source], recv_sem=twin_recv.at[source],
            device_id={"parts": 1 - part}, device_id_type=MESH,
        )

    def pass_on(s, carry):
        source = partner(s)

        @pl.when(ours(s))
        def _():
            forward_copy(2, s).wait_recv()
            twin_copy(source).start()

        return carry

    def await_twin(s, carry):
        source = partner(s)

        @pl.when(jnp.logical_not(ours(s)))
        def _():
            twin_copy(source).wait_recv()

        return carry

    def await_all(copy, kind):
        def step(s, carry):
            copy(kind, s).wait_recv()
            return carry

        lax.fori_loop(1, group, step, 0)

    low, high = pl.ds(0, LANES), pl.ds(LANES, LANES)
    await_all(forward_copy, 0)
    outer_forward(group, recv.at[0], lines, 0, low)
    await_all(forward_copy, 1)
    outer_forward(group, recv.at[1], lines, 0, high)
    load_f.wait()
    load_b.wait()

    def lag_step(k, carry):
        both = jnp.dot(table_f[k], lines[k], preferred_element_type=F32)
        spectra[k] = both
        g_re, g_im = both[:rows, :LANES], both[rows:, :LANES]
        m_re, m_im = both[:rows, LANES:], both[rows:, LANES:]
        product = jnp.concatenate(
            [g_re * m_re + g_im * m_im, g_im * m_re - g_re * m_im], axis=0
        ).astype(BF16)
        waves[k, :, low] = jnp.dot(table_b[k], product, preferred_element_type=F32)
        return carry

    lax.fori_loop(0, group, lag_step, 0, unroll=4)
    lax.fori_loop(1, group, pass_on, 0)
    outer_backward(group, waves, low, back.at[2])

    def return_all(kind, first=1, last=group):
        def step(s, carry):
            back_copy(kind, s).start()
            return carry

        lax.fori_loop(first, last, step, 0)

    return_all(2)

    lax.fori_loop(1, group, await_twin, 0)
    outer_forward(group, recv.at[2], lines, 0, low)

    def conv_step(k, carry):
        own = jnp.dot(table_f[k], lines[k, :, low], preferred_element_type=F32)
        l_re, l_im = own[:rows], own[rows:]
        both = spectra[k]
        g_re, g_im = both[:rows, :LANES], both[rows:, :LANES]
        m_re, m_im = both[:rows, LANES:], both[rows:, LANES:]
        grad_part = jnp.concatenate(
            [l_re * g_re + l_im * g_im, l_re * g_im - l_im * g_re], axis=0
        ).astype(BF16)
        conv_part = jnp.concatenate(
            [l_re * m_re - l_im * m_im, l_re * m_im + l_im * m_re], axis=0
        ).astype(BF16)
        product = jnp.concatenate([grad_part, conv_part], axis=1)
        waves[k] = jnp.dot(table_b[k], product, preferred_element_type=F32)
        return carry

    lax.fori_loop(0, group, conv_step, 0, unroll=4)
    outer_backward(group, waves, low, back.at[0])
    return_all(0)
    outer_backward(group, waves, high, back.at[1])
    return_all(1, 1, CUT_ONE)

    def keep_own(kind):
        home[kind, me] = back[kind, me]

    keep_own(2)
    keep_own(0)
    keep_own(1)

    await_all(back_copy, 2)

    def filter_step(p, carry):
        out_filter[:, cols(p)] = home[2, p].astype(F32) * envelope(p)
        return carry

    lax.fori_loop(0, group, filter_step, 0)

    await_all(back_copy, 0)

    def grad_step(p, carry):
        mixed_grad = home[0, p].astype(F32)
        out_key[:, cols(p)] = (mixed_grad * shaped[p].astype(F32)).astype(BF16)
        low_grad = (mixed_grad * key[:, cols(p)].astype(F32)).astype(BF16)
        shaped_grad[p] = low_grad
        line = low_grad.astype(F32)
        now, one, two = extended(p)
        sums = [jnp.sum(line * x, axis=0, keepdims=True) for x in (now, one, two)]
        tap_part[p] = jnp.concatenate(sums + [jnp.zeros((5, LANES), F32)], axis=0)
        return carry

    lax.fori_loop(0, group, grad_step, 0)
    rim_back = remote(
        shaped_grad.at[:, pl.ds(0, CHUNK), :], rim_grad, rim_send.at[1], rim_recv.at[1], left
    )
    rim_back.start()

    def tap_copy(s):
        peer = partner(s)
        return remote(tap_part.at[peer], tap_recv.at[me], tap_send.at[s], tap_rsem.at[s], peer)

    def sum_copy(s):
        peer = partner(s)
        return remote(tap_sum, tap_all.at[me], sum_send.at[s], sum_recv.at[s], peer)

    def loop(body):
        def step(s, carry):
            body(s)
            return carry

        lax.fori_loop(1, group, step, 0)

    loop(lambda s: tap_copy(s).start())
    return_all(1, CUT_ONE, CUT_TWO)
    tap_recv[me] = tap_part[me]

    def value_step(p, carry):
        rim = rim_grad[p].astype(F32)
        rim = jnp.where(me == group - 1, jnp.zeros_like(rim), rim)
        ext = jnp.concatenate([shaped_grad[p].astype(F32), rim], axis=0)
        weight = taps[:, cols(p)]
        total = weight[0:1] * ext[:rows] + weight[1:2] * ext[1 : rows + 1]
        out_value[:, cols(p)] = (total + weight[2:3] * ext[2 : rows + 2]).astype(BF16)
        return carry

    loop(lambda s: tap_copy(s).wait_recv())
    tap_sum[...] = jnp.sum(tap_recv[...], axis=0) * scale
    loop(lambda s: sum_copy(s).start())
    return_all(1, CUT_TWO, group)
    tap_all[me] = tap_sum[...]
    rim_back.wait_recv()
    lax.fori_loop(0, group, value_step, 0)

    await_all(back_copy, 1)

    def query_step(p, carry):
        conv = home[1, p].astype(F32)
        out_query[:, cols(p)] = (grad[:, cols(p)].astype(F32) * conv).astype(BF16)
        return carry

    lax.fori_loop(0, group, query_step, 0)
    loop(lambda s: sum_copy(s).wait_recv())
    for p in range(group):
        out_short[:, p * LANES : (p + 1) * LANES] = tap_all[p][0:3]

    def drain(s):
        for kind in range(2):
            forward_copy(kind, s).wait_send()
        for kind in range(3):
            back_copy(kind, s).wait_send()

        @pl.when(ours(s))
        def _():
            forward_copy(2, s).wait_send()
            twin_copy(partner(s)).wait_send()

        tap_copy(s).wait_send()
        sum_copy(s).wait_send()

    loop(drain)
    rim_copy.wait_send()
    rim_back.wait_send()


def deliver(results):
    count = len(results)
    steps = 4

    def body(*refs):
        for source, target in zip(refs[:count], refs[count:]):
            target[...] = source[...]

    def place(x):
        if x.shape[0] % (steps * CHUNK):
            return pl.BlockSpec(x.shape, lambda i: (0, 0))
        return pl.BlockSpec((x.shape[0] // steps, x.shape[1]), lambda i: (i, 0))

    places = [place(x) for x in results]
    return pl.pallas_call(
        body,
        grid=(steps,),
        out_shape=tuple(jax.ShapeDtypeStruct(x.shape, x.dtype) for x in results),
        in_specs=places,
        out_specs=tuple(places),
    )(*results)


def fused(group, query_in, key_in, value_in, grad_out, filter_raw, decay_rate, short_weight):
    rows, channels = query_in.shape
    table_f, table_b = inner_tables(group, rows)
    vmem = pl.BlockSpec(memory_space=pltpu.VMEM)
    blocks = (group, rows, LANES)
    dma = pltpu.SemaphoreType.DMA
    results = pl.pallas_call(
        functools.partial(kernel, group),
        out_shape=(
            jax.ShapeDtypeStruct((rows, channels), BF16),
            jax.ShapeDtypeStruct((rows, channels), BF16),
            jax.ShapeDtypeStruct((rows, channels), BF16),
            jax.ShapeDtypeStruct((rows, channels), F32),
            jax.ShapeDtypeStruct((3, channels), F32),
        ),
        in_specs=[vmem] * 7 + [pl.BlockSpec(memory_space=pl.ANY)] * 2,
        out_specs=(vmem,) * 5,
        scratch_shapes=[
            pltpu.VMEM(table_f.shape, BF16),
            pltpu.VMEM(table_b.shape, BF16),
            pltpu.VMEM((3,) + blocks, BF16),
            pltpu.VMEM((3,) + blocks, BF16),
            pltpu.VMEM(blocks, BF16),
            pltpu.VMEM((group, 2 * rows, 2 * LANES), BF16),
            pltpu.VMEM((group, 2 * rows, 2 * LANES), F32),
            pltpu.VMEM((group, 2 * rows, 2 * LANES), F32),
            pltpu.VMEM((3,) + blocks, BF16),
            pltpu.VMEM((3,) + blocks, BF16),
            pltpu.VMEM(blocks, BF16),
            pltpu.VMEM((CHUNK, channels), BF16),
            pltpu.VMEM((group, CHUNK, LANES), BF16),
            pltpu.VMEM((group, 8, LANES), F32),
            pltpu.VMEM((group, 8, LANES), F32),
            pltpu.VMEM((8, LANES), F32),
            pltpu.VMEM((group, 8, LANES), F32),
            dma((2,)),
            dma((3, group)),
            dma((3, group)),
            dma((3, group)),
            dma((3, group)),
            dma((2,)),
            dma((2,)),
            dma((group,)),
            dma((group,)),
            dma((group,)),
            dma((group,)),
            dma((group,)),
            dma((group,)),
        ],
        compiler_params=pltpu.CompilerParams(
            collective_id=0, has_side_effects=True, vmem_limit_bytes=56 * 2**20
        ),
    )(
        query_in, key_in, value_in, grad_out, filter_raw,
        decay_rate.reshape(1, channels), short_weight,
        jnp.asarray(table_f), jnp.asarray(table_b),
    )
    return deliver(results)


def shifted(block, axis, distance):
    devices = range(lax.axis_size(axis))
    route = [(i - distance, i) for i in devices if i - distance in devices]
    return lax.ppermute(block, axis, route)


def dft_tables(length):
    index_line = jnp.arange(length, dtype=jnp.int32)
    phase_int = index_line[:, None] * index_line[None, :] % length
    angles = phase_int.astype(jnp.float32) * (-2.0 * math.pi / length)
    return (jnp.cos(angles), jnp.sin(angles))


def twist_tables(outer_size, inner_size, length):
    outer_line = jnp.arange(outer_size, dtype=jnp.int32)
    inner_line = jnp.arange(inner_size, dtype=jnp.int32)
    phase_int = outer_line[:, None] * inner_line[None, :] % length
    angles = phase_int.astype(jnp.float32) * (-2.0 * math.pi / length)
    return (jnp.cos(angles), jnp.sin(angles))


def right_multiply(values, table):
    return jnp.einsum("ckn,nm->ckm", values, table, precision=HIGHEST)


def forward_transform(signal, tables):
    cos_outer, sin_outer, cos_inner, sin_inner, twist_cos, twist_sin = tables
    channels = signal.shape[0]
    half_rows = cos_outer.shape[0] // 2
    blocks = signal.reshape(channels, half_rows, cos_inner.shape[0])
    first_re = jnp.einsum("kn,cna->cka", cos_outer[:, :half_rows], blocks, precision=HIGHEST)
    first_im = jnp.einsum("kn,cna->cka", sin_outer[:, :half_rows], blocks, precision=HIGHEST)
    turned_re = first_re * twist_cos - first_im * twist_sin
    turned_im = first_re * twist_sin + first_im * twist_cos
    spec_re = right_multiply(turned_re, cos_inner) - right_multiply(turned_im, sin_inner)
    spec_im = right_multiply(turned_re, sin_inner) + right_multiply(turned_im, cos_inner)
    return (spec_re, spec_im)


def inverse_transform(spec_re, spec_im, tables):
    cos_outer, sin_outer, cos_inner, sin_inner, twist_cos, twist_sin = tables
    channels = spec_re.shape[0]
    half_rows = cos_outer.shape[0] // 2
    back_re = right_multiply(spec_re, cos_inner) + right_multiply(spec_im, sin_inner)
    back_im = right_multiply(spec_im, cos_inner) - right_multiply(spec_re, sin_inner)
    turned_re = back_re * twist_cos + back_im * twist_sin
    turned_im = back_im * twist_cos - back_re * twist_sin
    signal = jnp.einsum("nk,cka->cna", cos_outer[:half_rows], turned_re, precision=HIGHEST)
    signal = signal + jnp.einsum("nk,cka->cna", sin_outer[:half_rows], turned_im, precision=HIGHEST)
    scaled = signal * (1.0 / (cos_outer.shape[0] * cos_inner.shape[0]))
    return scaled.reshape(channels, -1)


def per_device(query_in, key_in, value_in, grad_out, filter_raw, decay_rate, short_weight):
    local_rows = query_in.shape[0]
    group_size = lax.axis_size("inner")
    seq_length = local_rows * group_size
    scale_factor = 1.0 / math.sqrt(seq_length)
    first_row = lax.axis_index("inner") * local_rows
    position = (first_row + jnp.arange(local_rows, dtype=jnp.int32)).astype(jnp.float32)
    envelope = jnp.exp(-decay_rate[None, :] * position[:, None] / seq_length) * scale_factor
    rim_rows = shifted(value_in[local_rows - 2 :], "inner", 1)
    extended = jnp.concatenate([rim_rows, value_in], axis=0).astype(jnp.float32)
    value_now = extended[2:]
    value_one = extended[1:-1]
    value_two = extended[:-2]
    shaped = (
        short_weight[0] * value_now + short_weight[1] * value_one + short_weight[2] * value_two
    ).astype(jnp.bfloat16)
    mixed = (key_in.astype(jnp.float32) * shaped.astype(jnp.float32)).astype(jnp.bfloat16)
    gated = (query_in.astype(jnp.float32) * grad_out.astype(jnp.float32)).astype(jnp.bfloat16)
    lagged = filter_raw * envelope
    mixed_half, gated_half = (
        lax.all_to_all(mixed.T, "inner", split_axis=0, concat_axis=1, tiled=True),
        lax.all_to_all(gated.T, "inner", split_axis=0, concat_axis=1, tiled=True),
    )
    filter_cols = lax.all_to_all(lagged.T, "inner", split_axis=0, concat_axis=1, tiled=True)
    mixed_cols = mixed_half.astype(jnp.float32)
    gated_cols = gated_half.astype(jnp.float32)
    fft_length = 2 * seq_length
    exponent = fft_length.bit_length() - 1
    inner_size = 2 ** (exponent // 2)
    outer_size = fft_length // inner_size
    cos_outer, sin_outer = dft_tables(outer_size)
    cos_inner, sin_inner = dft_tables(inner_size)
    twist_cos, twist_sin = twist_tables(outer_size, inner_size, fft_length)
    tables = (cos_outer, sin_outer, cos_inner, sin_inner, twist_cos, twist_sin)
    mix_re, mix_im = forward_transform(mixed_cols, tables)
    gate_re, gate_im = forward_transform(gated_cols, tables)
    filt_re, filt_im = forward_transform(filter_cols, tables)
    conv_cols = inverse_transform(
        filt_re * mix_re - filt_im * mix_im, filt_re * mix_im + filt_im * mix_re, tables
    )
    grad_cols = inverse_transform(
        filt_re * gate_re + filt_im * gate_im, filt_re * gate_im - filt_im * gate_re, tables
    )
    lag_cols = inverse_transform(
        gate_re * mix_re + gate_im * mix_im, gate_im * mix_re - gate_re * mix_im, tables
    )
    conv_low = conv_cols.astype(jnp.bfloat16)
    grad_low = grad_cols.astype(jnp.bfloat16)
    conv_rows, grad_rows = (
        lax.all_to_all(conv_low, "inner", split_axis=1, concat_axis=0, tiled=True),
        lax.all_to_all(grad_low, "inner", split_axis=1, concat_axis=0, tiled=True),
    )
    lag_rows = lax.all_to_all(lag_cols, "inner", split_axis=1, concat_axis=0, tiled=True)
    conv = conv_rows.T.astype(jnp.float32)
    grad_mixed = grad_rows.T.astype(jnp.float32)
    grad_lag = lag_rows.T
    grad_query = (grad_out.astype(jnp.float32) * conv).astype(jnp.bfloat16)
    grad_key = (grad_mixed * shaped.astype(jnp.float32)).astype(jnp.bfloat16)
    grad_shaped = (grad_mixed * key_in.astype(jnp.float32)).astype(jnp.bfloat16)
    next_rows = shifted(grad_shaped[:2], "inner", -1)
    grad_ext = jnp.concatenate([grad_shaped, next_rows], axis=0).astype(jnp.float32)
    grad_now = grad_ext[:local_rows]
    grad_one = grad_ext[1 : local_rows + 1]
    grad_two = grad_ext[2:]
    grad_value = (
        short_weight[0] * grad_now + short_weight[1] * grad_one + short_weight[2] * grad_two
    ).astype(jnp.bfloat16)
    partial_taps = jnp.stack(
        [
            jnp.sum(grad_now * value_now, axis=0),
            jnp.sum(grad_now * value_one, axis=0),
            jnp.sum(grad_now * value_two, axis=0),
        ]
    )
    grad_short = lax.psum(partial_taps, "inner") * scale_factor
    grad_filter = grad_lag * envelope
    return (grad_query, grad_key, grad_value, grad_filter, grad_short)


def dispatch(*arrays):
    rows, channels = arrays[0].shape
    group = lax.axis_size("inner")
    shape_fits = rows == LANES and group == 16 and channels == group * LANES
    if shape_fits and lax.axis_size("parts") == 2:
        return fused(group, *arrays)
    return per_device(*arrays)


def solution(mesh):
    in_specs = (
        P(("parts", "inner"), None),
        P(("parts", "inner"), None),
        P(("parts", "inner"), None),
        P(("parts", "inner"), None),
        P("inner", None),
        P(),
        P(),
    )
    out_specs = (
        P(("parts", "inner"), None),
        P(("parts", "inner"), None),
        P(("parts", "inner"), None),
        P(("parts", "inner"), None),
        P("parts", None),
    )
    return jax.shard_map(
        dispatch, mesh=mesh, in_specs=in_specs, out_specs=out_specs, check_vma=False
    )
```
